32 devices in a mesh: tm: 8 (over z, y), elec: 4 (over x, core).
Axes of the slice: x: 2, y: 2, z: 4, core: 2. Of those that a mesh axis runs over, the one named last changes fastest.
Arguments:
- signal: bfloat16 [16, 1024, 256], P('elec', 'tm'), may hold values from -16 to 16
- w_qkv: bfloat16 [256, 1152], replicated, may hold values from -0.375 to 0.375
- w_decay: bfloat16 [256, 4], replicated, may hold values from -0.375 to 0.375
- decay_rate: float32 [4], replicated, may hold values from 0.00048828125 to 0.05
- lin_gain: float32 [128], replicated, may hold values from 0.25 to 1.75
- w_out: bfloat16 [384, 256], replicated, may hold values from -0.3125 to 0.3125
- valid: int32 [16], replicated, may hold values 0 or 1
- boundary: int32 [1024], P('tm'), may hold values 0 or 1
Outputs:
- encoded: bfloat16 [16, 1024, 256], P('elec', 'tm')
The draws below stay inside these ranges and needn't reach their ends.
All inputs are finite; a program needn't handle non-finite values. No bound on the sum of `boundary` on one device may be relied on, other than what follows from the above.
Results may differ from the reference program's by a relative error of at most 0.006.
The reference program's roundings to bfloat16 on the way count: a program that leaves them out, or rounds other values in their place, can miss the bound.
Values may be sent and summed in bfloat16 or wider, within the bound.
A program may use at most 128 MiB of HBM per device.

```python
import math
import jax
import jax.numpy as jnp
from jax import lax

D = 256
H = 4
HD = 32
WIN = 128
P_DEV = 128
INNER = 128
EPOCH_COUNT = 1024
E = 16
N_TM = 8


def draw_signal(key, part):
    primary_random_draw = jax.random.fold_in(key, 0)
    payload_entries = jax.random.normal(primary_random_draw, (E, EPOCH_COUNT, D), jnp.float32)
    return jnp.clip(payload_entries, -16.0, 16.0).astype(jnp.bfloat16)


def plant(values, rng, low, top_value):
    place = [jax.random.randint(jax.random.fold_in(rng, axis), (), 0, length) for axis, length in enumerate(values.shape)]
    main_axis = values.shape.index(max(values.shape))
    next_to = place[:main_axis] + [(place[main_axis] + 1) % values.shape[main_axis]] + place[main_axis + 1:]
    return values.at[tuple(place)].set(low).at[tuple(next_to)].set(top_value)


def scatter_about(key, shape, width, most, kind=jnp.bfloat16):
    values = jax.random.normal(key, shape, jnp.float32) * width
    return jnp.minimum(jnp.maximum(values, -most), most).astype(kind)


def setup_inputs(seed: int = 0) -> dict:
    arg_keys = jax.random.split(jax.random.key(seed), 9)
    return {
        "signal": draw_signal(jax.random.fold_in(arg_keys[8], 71), 0),
        "w_qkv": scatter_about(arg_keys[1], (D, 9 * INNER), D ** -0.5, 0.375),
        "w_decay": scatter_about(arg_keys[2], (D, H), D ** -0.5, 0.375),
        "decay_rate": jnp.clip(jnp.exp(jax.random.uniform(arg_keys[3], (H,), jnp.float32, math.log(0.00048828125), math.log(0.05))), 0.00048828125, 0.05),
        "lin_gain": jnp.clip(1.0 + 0.15 * jax.random.normal(arg_keys[4], (INNER,), jnp.float32), 0.25, 1.75),
        "w_out": scatter_about(arg_keys[5], (3 * INNER, D), (3 * INNER) ** -0.5, 0.3125),
        "valid": plant((jax.random.randint(arg_keys[6], (E,), 0, 8) < 7).astype(jnp.int32), jax.random.fold_in(arg_keys[6], 1), 0, 1),
        "boundary": plant((jax.random.randint(arg_keys[7], (EPOCH_COUNT,), 0, P_DEV * N_TM) < 4).astype(jnp.int32), jax.random.fold_in(arg_keys[7], 1), 0, 1),
    }


def linear_local(query, keys, payload_entries, log_decay):
    head_dim = query.shape[-1]
    step_count = query.shape[1]
    cumulative = jnp.cumsum(log_decay, axis=1)
    by_head = jnp.transpose(cumulative, (0, 2, 1))
    spread = by_head[:, :, :, None] - by_head[:, :, None, :]
    positions = jnp.arange(step_count, dtype=jnp.int32)
    causal = positions[:, None] >= positions[None, :]
    decays = jnp.where(causal, jnp.exp(jnp.where(causal, spread, 0.0)), 0.0)
    scores = jnp.einsum('ethd,eshd->ehts', query.astype(jnp.float32), keys.astype(jnp.float32)) * head_dim ** (-0.5)
    weights = (scores * decays).astype(jnp.bfloat16)
    intra = jnp.einsum('ehts,eshd->ethd', weights.astype(jnp.float32), payload_entries.astype(jnp.float32))
    ending = cumulative[:, -1, :]
    kept = jnp.exp(ending[:, None, :] - cumulative)
    local_state = jnp.einsum('eshd,eshf->ehdf', keys.astype(jnp.float32) * kept[..., None], payload_entries.astype(jnp.float32), precision=lax.Precision.HIGHEST)
    return (intra, cumulative, jnp.exp(ending), local_state)

def carried_in(query, cumulative, state):
    head_dim = query.shape[-1]
    lifted = query.astype(jnp.float32) * (jnp.exp(cumulative) * head_dim ** (-0.5))[..., None]
    return jnp.einsum('ethd,ehdf->ethf', lifted, state, precision=lax.Precision.HIGHEST)

def window_attend(query, keys, payload_entries, query_start, key_start):
    elec_count, row_count, head_count, head_dim = query.shape
    key_count = keys.shape[1]
    query_pos = query_start + jnp.arange(row_count, dtype=jnp.int32)
    key_pos = key_start + jnp.arange(key_count, dtype=jnp.int32)
    allowed = (key_pos[None, :] <= query_pos[:, None]) & (key_pos[None, :] >= query_pos[:, None] - WIN) & (key_pos[None, :] >= 0)

    def one_head(triple):
        head_query, head_keys, head_values = triple
        scores = jnp.einsum('ebd,ekd->ebk', head_query.astype(jnp.float32), head_keys.astype(jnp.float32)) * head_dim ** (-0.5)
        masked = jnp.where(allowed[None], scores, -jnp.inf)
        row_peak = lax.optimization_barrier(jnp.max(masked, axis=-1))
        expweights = jnp.exp(jnp.where(allowed[None], scores - row_peak[..., None], -jnp.inf))
        totals = lax.optimization_barrier(jnp.sum(expweights, axis=-1))
        rounded = expweights.astype(jnp.bfloat16).astype(jnp.float32)
        return jnp.einsum('ebk,ekd->ebd', rounded, head_values.astype(jnp.float32)) / totals[..., None]
    outputs = lax.map(one_head, (jnp.transpose(query, (2, 0, 1, 3)), jnp.transpose(keys, (2, 0, 1, 3)), jnp.transpose(payload_entries, (2, 0, 1, 3))))
    return jnp.transpose(outputs, (1, 2, 0, 3)).reshape(elec_count, row_count, head_count * head_dim)

def electrode_attend(query, keys, payload_entries, valid):
    elec_count, row_count, inner_width = query.shape
    shape_four = (elec_count, row_count, H, HD)
    scores = jnp.einsum('ethd,jthd->thej', query.reshape(shape_four).astype(jnp.float32), keys.reshape(shape_four).astype(jnp.float32)) * HD ** (-0.5)
    positions = jnp.arange(elec_count, dtype=jnp.int32)
    allowed = (valid[None, :] == 1) | (positions[:, None] == positions[None, :])
    masked = jnp.where(allowed, scores, -jnp.inf)
    row_peak = lax.optimization_barrier(jnp.max(masked, axis=-1))
    expweights = jnp.exp(jnp.where(allowed, scores - row_peak[..., None], -jnp.inf))
    totals = lax.optimization_barrier(jnp.sum(expweights, axis=-1))
    rounded = expweights.astype(jnp.bfloat16).astype(jnp.float32)
    mixed_heads = jnp.einsum('thej,jthd->thed', rounded, payload_entries.reshape(shape_four).astype(jnp.float32)) / totals[..., None]
    return jnp.transpose(mixed_heads, (2, 0, 1, 3)).reshape(elec_count, row_count, inner_width)

def reference(signal, w_qkv, w_decay, decay_rate, lin_gain, w_out, valid, boundary):
    flat_rows = signal.reshape(E * EPOCH_COUNT, D)
    projected = jnp.dot(flat_rows, w_qkv, preferred_element_type=jnp.float32).astype(jnp.bfloat16)
    projected = projected.reshape(E, EPOCH_COUNT, 9, INNER)
    logits = jnp.dot(flat_rows, w_decay, preferred_element_type=jnp.float32).reshape(E, EPOCH_COUNT, H)
    log_decay = -2.0 * decay_rate * jax.nn.sigmoid(logits) + boundary[None, :, None].astype(jnp.float32) * math.log(0.5)
    blocks = EPOCH_COUNT // P_DEV

    def split_blocks(array):
        return jnp.swapaxes(array.reshape((E, blocks, P_DEV) + array.shape[2:]), 0, 1)
    shape_four = (E, EPOCH_COUNT, H, HD)

    def advance(state, inputs):
        block_query, block_keys, block_values, block_decay = inputs
        intra, cumulative, decay_all, local_state = linear_local(block_query, block_keys, block_values, block_decay)
        result = intra + carried_in(block_query, cumulative, state)
        new_state = decay_all[..., None, None] * state + local_state
        return (new_state, result)
    initial = jnp.zeros((E, H, HD, HD), jnp.float32)
    final_state, lin_blocks = lax.scan(advance, initial, (split_blocks(projected[:, :, 0].reshape(shape_four)), split_blocks(projected[:, :, 1].reshape(shape_four)), split_blocks(projected[:, :, 2].reshape(shape_four)), split_blocks(log_decay)))
    lin_raw = jnp.swapaxes(lin_blocks, 0, 1).reshape(E, EPOCH_COUNT, INNER)
    mean_square = lax.optimization_barrier(jnp.mean(lin_raw * lin_raw, axis=-1, keepdims=True))
    lin_out = lin_raw * lax.rsqrt(mean_square + 1e-05) * lin_gain
    padded_keys = jnp.concatenate([jnp.zeros((E, WIN, INNER), jnp.bfloat16), projected[:, :, 4]], axis=1)
    padded_values = jnp.concatenate([jnp.zeros((E, WIN, INNER), jnp.bfloat16), projected[:, :, 5]], axis=1)

    def window_block(block_index):
        begin = block_index * P_DEV
        block_query = lax.dynamic_slice_in_dim(projected[:, :, 3], begin, P_DEV, 1)
        block_keys = lax.dynamic_slice_in_dim(padded_keys, begin, P_DEV + WIN, 1)
        block_values = lax.dynamic_slice_in_dim(padded_values, begin, P_DEV + WIN, 1)
        return window_attend(block_query.reshape(E, P_DEV, H, HD), block_keys.reshape(E, P_DEV + WIN, H, HD), block_values.reshape(E, P_DEV + WIN, H, HD), begin, begin - WIN)
    win_blocks = lax.map(window_block, jnp.arange(blocks, dtype=jnp.int32))
    win_out = jnp.swapaxes(win_blocks, 0, 1).reshape(E, EPOCH_COUNT, INNER)

    def electrode_block(block_index):
        begin = block_index * P_DEV
        return electrode_attend(lax.dynamic_slice_in_dim(projected[:, :, 6], begin, P_DEV, 1), lax.dynamic_slice_in_dim(projected[:, :, 7], begin, P_DEV, 1), lax.dynamic_slice_in_dim(projected[:, :, 8], begin, P_DEV, 1), valid)
    ele_blocks = lax.map(electrode_block, jnp.arange(blocks, dtype=jnp.int32))
    ele_out = jnp.swapaxes(ele_blocks, 0, 1).reshape(E, EPOCH_COUNT, INNER)
    mixed = jnp.concatenate([lin_out, win_out, ele_out], axis=-1).astype(jnp.bfloat16)
    update = jnp.dot(mixed.reshape(E * EPOCH_COUNT, 3 * INNER), w_out, preferred_element_type=jnp.float32)
    return (flat_rows.astype(jnp.float32) + update).astype(jnp.bfloat16).reshape(E, EPOCH_COUNT, D)
```

```python
import functools
import math

import jax
import jax.numpy as jnp
from jax import lax
from jax.experimental import pallas as pl
from jax.experimental.pallas import tpu as pltpu
from jax.sharding import PartitionSpec as P

WIN = 128
HEADS = 4
INNER = 128
LOG2E = 1.0 / math.log(2.0)
F32 = jnp.float32
BF16 = jnp.bfloat16
MESH = pl.DeviceIdType.MESH
GROUP = 8


def dot(a, b):
    return jnp.dot(a, b, preferred_element_type=F32)


def dot_t(a, b):
    return lax.dot_general(a, b, (((1,), (1,)), ((), ())), preferred_element_type=F32)


def split(a):
    high = a.astype(BF16)
    return high, (a - high.astype(F32)).astype(BF16)


def iota(shape, dim):
    return lax.broadcasted_iota(jnp.int32, shape, dim)


def kernel(
    n_tm,
    chunks,
    sig_in,
    wqkv_in,
    wdec_ref,
    rate_ref,
    gain_ref,
    wout_in,
    valid_ref,
    bound_ref,
    out_ref,
    sig,
    wqkv,
    wout,
    wd,
    esig,
    wsig,
    proj,
    ekv,
    eq,
    cum_lanes,
    raw,
    ele,
    msg,
    got,
    local_sem,
    esend,
    erecv,
    wsend,
    wrecv,
    ssend,
    srecv,
):
    elecs, times, width = sig.shape
    hd = INNER // HEADS
    scale = hd**-0.5
    me = lax.axis_index("tm")
    who = lax.axis_index("elec")
    sib = who + 1 - 2 * lax.rem(who, 2)
    far = lax.rem(who + 2, 4)
    far_sib = lax.rem(sib + 2, 4)
    rounds = []
    step = 1
    while step < n_tm:
        rounds.append(step)
        step *= 2
    per = times // chunks

    local = [
        pltpu.make_async_copy(src, dst, local_sem.at[i])
        for i, (src, dst) in enumerate(((sig_in, sig), (wqkv_in, wqkv), (wout_in, wout)))
    ]
    for copy in local:
        copy.start()
    barrier = pltpu.get_barrier_semaphore()
    for peer in (sib, far):
        pl.semaphore_signal(barrier, inc=1, device_id={"elec": peer}, device_id_type=MESH)
    targets = 2
    for d in rounds:
        targets = targets + jnp.where(me + d < n_tm, 1, 0)

        @pl.when(me >= d)
        def _():
            pl.semaphore_signal(barrier, inc=1, device_id={"tm": me - d}, device_id_type=MESH)

    @pl.when(me == 0)
    def _():
        wsig[...] = jnp.zeros_like(wsig)

    for r, d in enumerate(rounds):

        @pl.when(me < d)
        def _():
            got[r, :, :hd, :] = jnp.zeros((elecs, hd, INNER), BF16)
            got[r, :, hd:, :] = jnp.ones((elecs, 16, INNER), BF16)

    wd[...] = jnp.zeros_like(wd)
    wd[:, :HEADS] = wdec_ref[...].astype(F32)

    def piece(slot, src, i, peer):
        span = pl.ds(i * per, per)
        return pltpu.make_async_remote_copy(
            src_ref=src.at[:, span, :],
            dst_ref=esig.at[slot, :, span, :],
            send_sem=esend.at[slot, i],
            recv_sem=erecv.at[slot, i],
            device_id={"elec": peer},
            device_id_type=MESH,
        )

    to_sib = [piece(0, sig, i, sib) for i in range(chunks)]
    to_far = [piece(1, sig, i, far) for i in range(chunks)]
    onward = [piece(2, esig.at[1], i, sib) for i in range(chunks)]
    to_next = [
        pltpu.make_async_remote_copy(
            src_ref=sig.at[e],
            dst_ref=wsig.at[e],
            send_sem=wsend.at[e],
            recv_sem=wrecv.at[e],
            device_id={"tm": me + 1},
            device_id_type=MESH,
        )
        for e in range(elecs)
    ]
    states = [
        pltpu.make_async_remote_copy(
            src_ref=msg.at[r],
            dst_ref=got.at[r],
            send_sem=ssend.at[r],
            recv_sem=srecv.at[r],
            device_id={"tm": me + d},
            device_id_type=MESH,
        )
        for r, d in enumerate(rounds)
    ]

    local[0].wait()
    pl.semaphore_wait(barrier, targets)
    for i in range(chunks):
        to_far[i].start()

    @pl.when(me + 1 < n_tm)
    def _():
        for copy in to_next:
            copy.start()

    for i in range(chunks):
        to_sib[i].start()
    local[1].wait()

    row = iota((times, INNER), 0)
    lane = iota((times, INNER), 1)
    causal = row >= lane
    lane_head = lane // hd
    flat = sig[...].reshape(elecs * times, width)
    logits_all = dot(flat, wd[...].astype(BF16))
    logits = logits_all[:times]
    for e in range(1, elecs):
        logits = logits + pltpu.roll(logits_all[e * times : (e + 1) * times], HEADS * e, 1)
    which = lax.rem(iota((1, INNER), 1), HEADS)
    rates = jnp.zeros((1, INNER), F32)
    for h in range(HEADS):
        rates = jnp.where(which == h, rate_ref[h], rates)
    soft = -2.0 * rates * jax.nn.sigmoid(logits)
    tri = jnp.where(causal, 1.0, 0.0)
    marks = jnp.where(causal, bound_ref[...].reshape(1, times).astype(F32), 0.0).astype(BF16)
    tri16 = tri.astype(BF16)
    soft_hi, soft_mid = split(soft)
    soft_lo = (soft - soft_hi.astype(F32) - soft_mid.astype(F32)).astype(BF16)
    bounds = dot(marks, jnp.ones((times, INNER), BF16))
    cum = dot(tri16, soft_hi) + dot(tri16, soft_mid) + dot(tri16, soft_lo) + math.log(0.5) * bounds
    cum2 = cum * LOG2E
    cum2_t = cum2.T
    proj[:, :, :384] = dot(flat, wqkv[:, :384]).astype(BF16).reshape(elecs, times, 384)

    block_diag = (row // hd) == lane_head
    inc_state, inc_dec = [], []
    for e in range(elecs):
        spread = jnp.broadcast_to(cum2[:, HEADS * e : HEADS * e + 1], (times, INNER))
        for h in range(1, HEADS):
            at = HEADS * e + h
            spread = jnp.where(
                lane_head == h, jnp.broadcast_to(cum2[:, at : at + 1], (times, INNER)), spread
            )
        cum_lanes[e] = spread
        ending = spread[times - 1 : times, :]
        kept = jnp.exp2(ending - spread)
        high, low = split((proj[e, :, 128:256].astype(F32) * kept).T)
        values = proj[e, :, 256:384]
        full = jnp.where(block_diag, dot(high, values) + dot(low, values), 0.0)
        small = full[:hd]
        for h in range(1, HEADS):
            small = small + full[h * hd : (h + 1) * hd]
        inc_state.append(small)
        inc_dec.append(jnp.exp2(ending))
    exc_state = [jnp.zeros((hd, INNER), F32)] * elecs
    exc_dec = [jnp.ones((1, INNER), F32)] * elecs

    def send_states(r, d):
        for e in range(elecs):
            msg[r, e, :hd, :] = inc_state[e].astype(BF16)
            msg[r, e, hd:, :] = jnp.broadcast_to(inc_dec[e], (16, INNER)).astype(BF16)

        @pl.when(me + d < n_tm)
        def _():
            states[r].start()

    def take_states(r, d):
        @pl.when(me >= d)
        def _():
            states[r].wait_recv()

        for e in range(elecs):
            came = got[r, e, :hd, :].astype(F32)
            dec = got[r, e, hd:, :].astype(F32)[:1]
            exc_state[e] = exc_dec[e] * came + exc_state[e]
            exc_dec[e] = exc_dec[e] * dec
            inc_state[e] = inc_dec[e] * came + inc_state[e]
            inc_dec[e] = inc_dec[e] * dec
        if r + 1 < len(rounds):
            send_states(r + 1, rounds[r + 1])

    send_states(0, rounds[0])

    proj[:, :, 384:768] = dot(flat, wqkv[:, 384:768]).astype(BF16).reshape(elecs, times, 384)
    own = dot(flat, wqkv[:, 768:1152]).astype(BF16).astype(F32).reshape(elecs, times, 384)
    eq[...] = own[:, :, :128]
    ekv[...] = own[:, :, 128:]

    head_row = iota((1, INNER), 1) // hd
    head_masks = [jnp.where(head_row == h, 1.0, 0.0) for h in range(HEADS)]
    masks16 = [m.astype(BF16) for m in head_masks]

    def by_head(query):
        return jnp.concatenate([query * m for m in masks16], axis=0)

    def pick(stacked, rows):
        head = iota((rows, INNER), 1) // hd
        result = stacked[:rows]
        for h in range(1, HEADS):
            result = jnp.where(head == h, stacked[h * rows : (h + 1) * rows], result)
        return result

    def linear(e):
        scores = dot_t(by_head(proj[e, :, :128]), proj[e, :, 128:256])
        weights = []
        for h in range(HEADS):
            at = HEADS * e + h
            gap = cum2[:, at : at + 1] - cum2_t[at : at + 1, :]
            decays = jnp.exp2(jnp.where(causal, gap, -jnp.inf))
            weights.append((scores[h * times : (h + 1) * times] * scale * decays).astype(BF16))
        raw[e] = pick(dot(jnp.concatenate(weights, axis=0), proj[e, :, 256:384]), times)

    fold = scale * LOG2E
    neg = -jnp.inf
    ones_keys = jnp.ones((2 * times, INNER), BF16)

    def window(e):
        @pl.when(me >= 1)
        def _():
            to_next[e].wait_recv()

        prior = dot(wsig[e], wqkv[:, 512:768]).astype(BF16)
        keys = jnp.concatenate([prior[:, :128], proj[e, :, 512:640]], axis=0)
        values = jnp.concatenate([prior[:, 128:], proj[e, :, 640:768]], axis=0)
        scores = dot_t(by_head(proj[e, :, 384:512]), keys)
        before = (lane >= row) & (me > 0)
        weights = []
        for h in range(HEADS):
            part = scores[h * times : (h + 1) * times]
            old = jnp.where(before, part[:, :times], neg)
            new = jnp.where(causal, part[:, times:], neg)
            peak = jnp.max(jnp.maximum(old, new), axis=1, keepdims=True)
            weights.append(
                jnp.concatenate(
                    [
                        jnp.exp2((old - peak) * fold).astype(BF16),
                        jnp.exp2((new - peak) * fold).astype(BF16),
                    ],
                    axis=1,
                )
            )
        both = dot(
            jnp.concatenate(weights, axis=0), jnp.concatenate([values, ones_keys], axis=1)
        )
        return pick(both[:, :128], times) / pick(both[:, 128:], times)

    qrows = elecs * GROUP
    krows = 4 * elecs * GROUP
    erow = iota((HEADS * qrows, krows), 0)
    ecol = iota((HEADS * qrows, krows), 1)
    good = jnp.zeros((1, krows), jnp.int32)
    col_elec = iota((1, krows), 1) // GROUP
    for slot, peer in enumerate((who, sib, far, far_sib)):
        for i in range(elecs):
            good = jnp.where(col_elec == slot * elecs + i, valid_ref[peer * elecs + i], good)
    eallowed = (lax.rem(erow, GROUP) == lax.rem(ecol, GROUP)) & (
        (jnp.broadcast_to(good, ecol.shape) == 1)
        | (ecol // GROUP == lax.rem(erow // GROUP, elecs))
    )
    ones_ele = jnp.ones((krows, INNER), BF16)

    def electrode(i):
        span = pl.ds(i * per, per)
        there = esig[:, :, span, :].reshape(3 * elecs * per, width)
        kv = dot(there, wqkv[:, 896:1152]).astype(BF16).astype(F32)
        kv = kv.reshape(3 * elecs, per, 256)
        for g in range(per // GROUP):
            begin = i * per + g * GROUP
            mine = ekv[:, begin : begin + GROUP, :].reshape(qrows, 256)
            rest = kv[:, g * GROUP : (g + 1) * GROUP, :].reshape(krows - qrows, 256)
            pair = jnp.concatenate([mine, rest], axis=0).astype(BF16)
            query = eq[:, begin : begin + GROUP, :].reshape(qrows, 128).astype(BF16)
            scores = jnp.where(eallowed, dot_t(by_head(query), pair[:, :128]), neg)
            peak = jnp.max(scores, axis=1, keepdims=True)
            weights = jnp.exp2((scores - peak) * fold).astype(BF16)
            both = dot(weights, jnp.concatenate([pair[:, 128:], ones_ele], axis=1))
            result = pick(both[:, :128], qrows) / pick(both[:, 128:], qrows)
            ele[:, begin : begin + GROUP, :] = result.reshape(elecs, GROUP, INNER)

    def forward(i):
        to_far[i].wait_recv()
        onward[i].start()

    linear(0)
    linear(1)
    take_states(0, rounds[0])
    linear(2)
    linear(3)
    forward(0)
    if len(rounds) > 1:
        take_states(1, rounds[1])
    win = [window(0)]
    forward(1)
    to_sib[0].wait_recv()
    onward[0].wait_recv()
    electrode(0)
    if len(rounds) > 2:
        take_states(2, rounds[2])
    win.append(window(1))
    forward(2)
    to_sib[1].wait_recv()
    onward[1].wait_recv()
    electrode(1)
    win.append(window(2))
    forward(3)
    to_sib[2].wait_recv()
    onward[2].wait_recv()
    electrode(2)
    win.append(window(3))
    for r in range(3, len(rounds)):
        take_states(r, rounds[r])
    gain = gain_ref[...].reshape(1, INNER)
    lin = []
    for e in range(elecs):
        tiled = jnp.concatenate([exc_state[e]] * HEADS, axis=0)
        s_hi, s_lo = split(jnp.where(block_diag, tiled, 0.0))
        q_hi, q_lo = split(proj[e, :, :128].astype(F32) * (jnp.exp2(cum_lanes[e]) * scale))
        total = raw[e] + dot(q_hi, s_hi) + dot(q_hi, s_lo) + dot(q_lo, s_hi)
        square = jnp.mean(total * total, axis=1, keepdims=True)
        lin.append((total * lax.rsqrt(square + 1e-05) * gain).astype(BF16))
    to_sib[3].wait_recv()
    onward[3].wait_recv()
    electrode(3)
    local[2].wait()
    for e in range(elecs):
        mixed = jnp.concatenate([lin[e], win[e].astype(BF16), ele[e].astype(BF16)], axis=1)
        out_ref[e] = (sig[e].astype(F32) + dot(mixed, wout[...])).astype(BF16)

    for copy in to_sib + to_far + onward:
        copy.wait_send()

    @pl.when(me + 1 < n_tm)
    def _():
        for copy in to_next:
            copy.wait_send()

    for r, d in enumerate(rounds):

        @pl.when(me + d < n_tm)
        def _():
            states[r].wait_send()


def shards(n_tm, signal, w_qkv, w_decay, decay_rate, lin_gain, w_out, valid, boundary):
    elecs, times, width = signal.shape
    hd = INNER // HEADS
    rounds = max(1, (n_tm - 1).bit_length())
    chunks = 4
    anywhere = pl.BlockSpec(memory_space=pl.ANY)
    vmem = pl.BlockSpec(memory_space=pltpu.VMEM)
    smem = pl.BlockSpec(memory_space=pltpu.SMEM)
    dma = pltpu.SemaphoreType.DMA
    return pl.pallas_call(
        functools.partial(kernel, n_tm, chunks),
        out_shape=jax.ShapeDtypeStruct(signal.shape, BF16),
        in_specs=[anywhere, anywhere, vmem, smem, vmem, anywhere, smem, vmem],
        out_specs=vmem,
        scratch_shapes=[
            pltpu.VMEM(signal.shape, BF16),
            pltpu.VMEM(w_qkv.shape, BF16),
            pltpu.VMEM(w_out.shape, BF16),
            pltpu.VMEM((width, INNER), F32),
            pltpu.VMEM((3, elecs, times, width), BF16),
            pltpu.VMEM((elecs, times, width), BF16),
            pltpu.VMEM((elecs, times, 768), BF16),
            pltpu.VMEM((elecs, times, 256), F32),
            pltpu.VMEM((elecs, times, INNER), F32),
            pltpu.VMEM((elecs, times, INNER), F32),
            pltpu.VMEM((elecs, times, INNER), F32),
            pltpu.VMEM((elecs, times, INNER), F32),
            pltpu.VMEM((rounds, elecs, hd + 16, INNER), BF16),
            pltpu.VMEM((rounds, elecs, hd + 16, INNER), BF16),
            dma((3,)),
            dma((3, chunks)),
            dma((3, chunks)),
            dma((elecs,)),
            dma((elecs,)),
            dma((rounds,)),
            dma((rounds,)),
        ],
        compiler_params=pltpu.CompilerParams(
            collective_id=0, has_side_effects=True, vmem_limit_bytes=48 * 2**20
        ),
    )(signal, w_qkv, w_decay, decay_rate, lin_gain, w_out, valid, boundary)


def solution(mesh):
    return jax.shard_map(
        functools.partial(shards, mesh.shape["tm"]),
        mesh=mesh,
        in_specs=(P("elec", "tm", None), P(), P(), P(), P(), P(), P(), P("tm")),
        out_specs=P("elec", "tm", None),
        check_vma=False,
    )
```

```python
import functools
import math

import jax
import jax.numpy as jnp
from jax import lax
from jax.experimental import pallas as pl
from jax.experimental.pallas import tpu as pltpu
from jax.sharding import PartitionSpec as P

WIN = 128
HEADS = 4
INNER = 128
LOG2E = 1.0 / math.log(2.0)
F32 = jnp.float32
BF16 = jnp.bfloat16
MESH = pl.DeviceIdType.MESH
GROUP = 8
EARLY = 1


def dot(a, b):
    return jnp.dot(a, b, preferred_element_type=F32)


def dot_t(a, b):
    return lax.dot_general(a, b, (((1,), (1,)), ((), ())), preferred_element_type=F32)


def split(a):
    high = a.astype(BF16)
    return high, (a - high.astype(F32)).astype(BF16)


def iota(shape, dim):
    return lax.broadcasted_iota(jnp.int32, shape, dim)


def kernel(
    n_tm,
    chunks,
    sig_in,
    wqkv_in,
    wdec_in,
    rate_in,
    gain_in,
    wout_in,
    valid_in,
    bound_in,
    out_ref,
    sig,
    wqkv,
    wout,
    wdec_ref,
    rate_ref,
    gain_ref,
    valid_ref,
    bound_ref,
    wd,
    esig,
    wsig,
    proj,
    ekv,
    eq,
    cum_lanes,
    raw,
    ele,
    msg,
    got,
    local_sem,
    esend,
    erecv,
    wsend,
    wrecv,
    ssend,
    srecv,
):
    elecs, times, width = sig.shape
    hd = INNER // HEADS
    scale = hd**-0.5
    me = lax.axis_index("tm")
    who = lax.axis_index("elec")
    sib = who + 1 - 2 * lax.rem(who, 2)
    far = lax.rem(who + 2, 4)
    far_sib = lax.rem(sib + 2, 4)
    rounds = []
    step = 1
    while step < n_tm:
        rounds.append(step)
        step *= 2
    per = times // chunks

    local = [
        pltpu.make_async_copy(src, dst, local_sem.at[i])
        for i, (src, dst) in enumerate(
            (
                (sig_in, sig),
                (wqkv_in, wqkv),
                (wout_in, wout),
                (wdec_in, wdec_ref),
                (rate_in, rate_ref),
                (gain_in, gain_ref),
                (valid_in, valid_ref),
                (bound_in, bound_ref),
            )
        )
    ]
    for copy in local:
        copy.start()
    barrier = pltpu.get_barrier_semaphore()
    for peer in (sib, far):
        pl.semaphore_signal(barrier, inc=1, device_id={"elec": peer}, device_id_type=MESH)
    targets = 2
    for d in rounds:
        targets = targets + jnp.where(me + d < n_tm, 1, 0)

        @pl.when(me >= d)
        def _():
            pl.semaphore_signal(barrier, inc=1, device_id={"tm": me - d}, device_id_type=MESH)

    @pl.when(me == 0)
    def _():
        wsig[...] = jnp.zeros_like(wsig)

    for r, d in enumerate(rounds):

        @pl.when(me < d)
        def _():
            got[r, : elecs * hd, :] = jnp.zeros((elecs * hd, INNER), BF16)
            got[r, elecs * hd :, :] = jnp.ones((16, INNER), BF16)

    wd[...] = jnp.zeros_like(wd)

    def piece(slot, src, i, peer):
        span = pl.ds(i * per, per)
        return pltpu.make_async_remote_copy(
            src_ref=src.at[:, span, :],
            dst_ref=esig.at[slot, :, span, :],
            send_sem=esend.at[slot, i],
            recv_sem=erecv.at[slot, i],
            device_id={"elec": peer},
            device_id_type=MESH,
        )

    to_sib = [piece(0, sig, i, sib) for i in range(chunks)]
    to_far = [piece(1, sig, i, far) for i in range(chunks)]
    onward = [piece(2, esig.at[1], i, sib) for i in range(chunks)]
    to_next = [
        pltpu.make_async_remote_copy(
            src_ref=sig.at[e],
            dst_ref=wsig.at[e],
            send_sem=wsend.at[e],
            recv_sem=wrecv.at[e],
            device_id={"tm": me + 1},
            device_id_type=MESH,
        )
        for e in range(elecs)
    ]
    states = [
        pltpu.make_async_remote_copy(
            src_ref=msg.at[r],
            dst_ref=got.at[r],
            send_sem=ssend.at[r],
            recv_sem=srecv.at[r],
            device_id={"tm": me + d},
            device_id_type=MESH,
        )
        for r, d in enumerate(rounds)
    ]

    for i in (0, 3, 4, 5, 6, 7):
        local[i].wait()
    wd[:HEADS, :] = wdec_ref[...].astype(F32)

    row = iota((times, INNER), 0)
    lane = iota((times, INNER), 1)
    causal = row >= lane
    lane_head = lane // hd
    flat = sig[...].reshape(elecs * times, width)
    logits_all = dot_t(flat, wd[...].astype(BF16))
    logits = logits_all[:times]
    for e in range(1, elecs):
        logits = logits + pltpu.roll(logits_all[e * times : (e + 1) * times], HEADS * e, 1)
    which = lax.rem(iota((1, INNER), 1), HEADS)
    rates = jnp.zeros((1, INNER), F32)
    for h in range(HEADS):
        rates = jnp.where(which == h, rate_ref[h], rates)
    soft = -2.0 * rates * jax.nn.sigmoid(logits)
    tri = jnp.where(causal, 1.0, 0.0)
    marks = jnp.where(causal, bound_ref[...].reshape(1, times).astype(F32), 0.0).astype(BF16)
    tri16 = tri.astype(BF16)
    soft_hi, soft_mid = split(soft)
    soft_lo = (soft - soft_hi.astype(F32) - soft_mid.astype(F32)).astype(BF16)
    bounds = dot(marks, jnp.ones((times, INNER), BF16))
    cum = dot(tri16, soft_hi) + dot(tri16, soft_mid) + dot(tri16, soft_lo) + math.log(0.5) * bounds
    cum2 = cum * LOG2E
    cum2_t = cum2.T
    pl.semaphore_wait(barrier, targets)
    for i in range(chunks):
        to_far[i].start()
    for i in range(chunks):
        to_sib[i].start()

    def send_window(first, last):
        @pl.when(me + 1 < n_tm)
        def _():
            for copy in to_next[first:last]:
                copy.start()

    send_window(0, EARLY)
    local[1].wait()
    proj[:, :, :384] = dot(flat, wqkv[:, :384]).astype(BF16).reshape(elecs, times, 384)

    block_diag = (row // hd) == lane_head
    inc_state, inc_dec = [], []
    for e in range(elecs):
        spread = jnp.broadcast_to(cum2[:, HEADS * e : HEADS * e + 1], (times, INNER))
        for h in range(1, HEADS):
            at = HEADS * e + h
            spread = jnp.where(
                lane_head == h, jnp.broadcast_to(cum2[:, at : at + 1], (times, INNER)), spread
            )
        cum_lanes[e] = spread
        ending = spread[times - 1 : times, :]
        kept = jnp.exp2(ending - spread)
        high, low = split((proj[e, :, 128:256].astype(F32) * kept).T)
        values = proj[e, :, 256:384]
        full = jnp.where(block_diag, dot(high, values) + dot(low, values), 0.0)
        small = full[:hd]
        for h in range(1, HEADS):
            small = small + full[h * hd : (h + 1) * hd]
        inc_state.append(small)
        inc_dec.append(jnp.exp2(ending))
    exc_state = [jnp.zeros((hd, INNER), F32)] * elecs
    exc_dec = [jnp.ones((1, INNER), F32)] * elecs

    def send_states(r, d):
        for e in range(elecs):
            msg[r, e * hd : (e + 1) * hd, :] = inc_state[e].astype(BF16)
        packed = jnp.broadcast_to(inc_dec[0], (16, INNER))
        for e in range(1, elecs):
            packed = jnp.where(iota((16, INNER), 0) == e, inc_dec[e], packed)
        msg[r, elecs * hd :, :] = packed.astype(BF16)

        @pl.when(me + d < n_tm)
        def _():
            states[r].start()

    def take_states(r, d):
        @pl.when(me >= d)
        def _():
            states[r].wait_recv()

        decs = got[r, elecs * hd :, :].astype(F32)
        for e in range(elecs):
            came = got[r, e * hd : (e + 1) * hd, :].astype(F32)
            dec = decs[e : e + 1]
            exc_state[e] = exc_dec[e] * came + exc_state[e]
            exc_dec[e] = exc_dec[e] * dec
            inc_state[e] = inc_dec[e] * came + inc_state[e]
            inc_dec[e] = inc_dec[e] * dec
        if r + 1 < len(rounds):
            send_states(r + 1, rounds[r + 1])

    send_states(0, rounds[0])
    send_window(EARLY, elecs)

    proj[:, :, 384:768] = dot(flat, wqkv[:, 384:768]).astype(BF16).reshape(elecs, times, 384)
    own = dot(flat, wqkv[:, 768:1152]).astype(BF16).astype(F32).reshape(elecs, times, 384)
    eq[...] = own[:, :, :128]
    ekv[...] = own[:, :, 128:]

    head_row = iota((1, INNER), 1) // hd
    head_masks = [jnp.where(head_row == h, 1.0, 0.0) for h in range(HEADS)]
    masks16 = [m.astype(BF16) for m in head_masks]

    def by_head(query):
        return jnp.concatenate([query * m for m in masks16], axis=0)

    def pick(stacked, rows):
        head = iota((rows, INNER), 1) // hd
        result = stacked[:rows]
        for h in range(1, HEADS):
            result = jnp.where(head == h, stacked[h * rows : (h + 1) * rows], result)
        return result

    def linear(e):
        scores = dot_t(by_head(proj[e, :, :128]), proj[e, :, 128:256])
        weights = []
        for h in range(HEADS):
            at = HEADS * e + h
            gap = cum2[:, at : at + 1] - cum2_t[at : at + 1, :]
            decays = jnp.exp2(jnp.where(causal, gap, -jnp.inf))
            weights.append((scores[h * times : (h + 1) * times] * scale * decays).astype(BF16))
        raw[e] = pick(dot(jnp.concatenate(weights, axis=0), proj[e, :, 256:384]), times)

    fold = scale * LOG2E
    neg = -jnp.inf
    ones_keys = jnp.ones((2 * times, INNER), BF16)

    def window(e):
        @pl.when(me >= 1)
        def _():
            to_next[e].wait_recv()

        prior = dot(wsig[e], wqkv[:, 512:768]).astype(BF16)
        keys = jnp.concatenate([prior[:, :128], proj[e, :, 512:640]], axis=0)
        values = jnp.concatenate([prior[:, 128:], proj[e, :, 640:768]], axis=0)
        scores = dot_t(by_head(proj[e, :, 384:512]), keys)
        before = (lane >= row) & (me > 0)
        weights = []
        for h in range(HEADS):
            part = scores[h * times : (h + 1) * times]
            old = jnp.where(before, part[:, :times], neg)
            new = jnp.where(causal, part[:, times:], neg)
            peak = jnp.max(jnp.maximum(old, new), axis=1, keepdims=True)
            weights.append(
                jnp.concatenate(
                    [
                        jnp.exp2((old - peak) * fold).astype(BF16),
                        jnp.exp2((new - peak) * fold).astype(BF16),
                    ],
                    axis=1,
                )
            )
        both = dot(
            jnp.concatenate(weights, axis=0), jnp.concatenate([values, ones_keys], axis=1)
        )
        return pick(both[:, :128], times) / pick(both[:, 128:], times)

    qrows = elecs * GROUP
    krows = 4 * elecs * GROUP
    erow = iota((HEADS * qrows, krows), 0)
    ecol = iota((HEADS * qrows, krows), 1)
    good = jnp.zeros((1, krows), jnp.int32)
    col_elec = iota((1, krows), 1) // GROUP
    for slot, peer in enumerate((who, sib, far, far_sib)):
        for i in range(elecs):
            good = jnp.where(col_elec == slot * elecs + i, valid_ref[peer * elecs + i], good)
    eallowed = (lax.rem(erow, GROUP) == lax.rem(ecol, GROUP)) & (
        (jnp.broadcast_to(good, ecol.shape) == 1)
        | (ecol // GROUP == lax.rem(erow // GROUP, elecs))
    )
    ones_ele = jnp.ones((krows, INNER), BF16)

    def electrode(i):
        span = pl.ds(i * per, per)
        there = esig[:, :, span, :].reshape(3 * elecs * per, width)
        kv = dot(there, wqkv[:, 896:1152]).astype(BF16).astype(F32)
        kv = kv.reshape(3 * elecs, per, 256)
        for g in range(per // GROUP):
            begin = i * per + g * GROUP
            mine = ekv[:, begin : begin + GROUP, :].reshape(qrows, 256)
            rest = kv[:, g * GROUP : (g + 1) * GROUP, :].reshape(krows - qrows, 256)
            pair = jnp.concatenate([mine, rest], axis=0).astype(BF16)
            query = eq[:, begin : begin + GROUP, :].reshape(qrows, 128).astype(BF16)
            scores = jnp.where(eallowed, dot_t(by_head(query), pair[:, :128]), neg)
            peak = jnp.max(scores, axis=1, keepdims=True)
            weights = jnp.exp2((scores - peak) * fold).astype(BF16)
            both = dot(weights, jnp.concatenate([pair[:, 128:], ones_ele], axis=1))
            result = pick(both[:, :128], qrows) / pick(both[:, 128:], qrows)
            ele[:, begin : begin + GROUP, :] = result.reshape(elecs, GROUP, INNER)

    def forward(i):
        to_far[i].wait_recv()
        onward[i].start()

    def attend(i):
        to_sib[i].wait_recv()
        onward[i].wait_recv()
        electrode(i)

    win = []
    linear(0)
    linear(1)
    forward(0)
    linear(2)
    forward(1)
    linear(3)
    take_states(0, rounds[0])
    win.append(window(0))
    attend(0)
    forward(2)
    if len(rounds) > 1:
        take_states(1, rounds[1])
    win.append(window(1))
    attend(1)
    forward(3)
    win.append(window(2))
    attend(2)
    win.append(window(3))
    for r in range(2, len(rounds)):
        take_states(r, rounds[r])
    gain = gain_ref[...].reshape(1, INNER)
    lin = []
    for e in range(elecs):
        tiled = jnp.concatenate([exc_state[e]] * HEADS, axis=0)
        s_hi, s_lo = split(jnp.where(block_diag, tiled, 0.0))
        q_hi, q_lo = split(proj[e, :, :128].astype(F32) * (jnp.exp2(cum_lanes[e]) * scale))
        total = raw[e] + dot(q_hi, s_hi) + dot(q_hi, s_lo) + dot(q_lo, s_hi)
        square = jnp.mean(total * total, axis=1, keepdims=True)
        lin.append((total * lax.rsqrt(square + 1e-05) * gain).astype(BF16))
    attend(3)
    local[2].wait()
    for e in range(elecs):
        mixed = jnp.concatenate([lin[e], win[e].astype(BF16), ele[e].astype(BF16)], axis=1)
        out_ref[e] = (sig[e].astype(F32) + dot(mixed, wout[...])).astype(BF16)

    for copy in to_sib + to_far + onward:
        copy.wait_send()

    @pl.when(me + 1 < n_tm)
    def _():
        for copy in to_next:
            copy.wait_send()

    for r, d in enumerate(rounds):

        @pl.when(me + d < n_tm)
        def _():
            states[r].wait_send()


def shards(n_tm, signal, w_qkv, w_decay, decay_rate, lin_gain, w_out, valid, boundary):
    elecs, times, width = signal.shape
    hd = INNER // HEADS
    rounds = max(1, (n_tm - 1).bit_length())
    chunks = 4
    hbm = pl.BlockSpec(memory_space=pltpu.HBM)
    dma = pltpu.SemaphoreType.DMA
    return pl.pallas_call(
        functools.partial(kernel, n_tm, chunks),
        out_shape=jax.ShapeDtypeStruct(signal.shape, BF16),
        in_specs=[hbm] * 8,
        out_specs=pl.BlockSpec(memory_space=pltpu.VMEM),
        scratch_shapes=[
            pltpu.VMEM(signal.shape, BF16),
            pltpu.VMEM(w_qkv.shape, BF16),
            pltpu.VMEM(w_out.shape, BF16),
            pltpu.VMEM((HEADS, width), BF16),
            pltpu.SMEM(decay_rate.shape, F32),
            pltpu.VMEM(lin_gain.shape, F32),
            pltpu.SMEM(valid.shape, jnp.int32),
            pltpu.VMEM(boundary.shape, jnp.int32),
            pltpu.VMEM((INNER, width), F32),
            pltpu.VMEM((3, elecs, times, width), BF16),
            pltpu.VMEM((elecs, times, width), BF16),
            pltpu.VMEM((elecs, times, 768), BF16),
            pltpu.VMEM((elecs, times, 256), F32),
            pltpu.VMEM((elecs, times, INNER), F32),
            pltpu.VMEM((elecs, times, INNER), F32),
            pltpu.VMEM((elecs, times, INNER), F32),
            pltpu.VMEM((elecs, times, INNER), F32),
            pltpu.VMEM((rounds, elecs * hd + 16, INNER), BF16),
            pltpu.VMEM((rounds, elecs * hd + 16, INNER), BF16),
            dma((8,)),
            dma((3, chunks)),
            dma((3, chunks)),
            dma((elecs,)),
            dma((elecs,)),
            dma((rounds,)),
            dma((rounds,)),
        ],
        compiler_params=pltpu.CompilerParams(
            collective_id=0, has_side_effects=True
        ),
    )(signal, w_qkv, w_decay.T, decay_rate, lin_gain, w_out, valid, boundary)


def solution(mesh):
    return jax.shard_map(
        functools.partial(shards, mesh.shape["tm"]),
        mesh=mesh,
        in_specs=(P("elec", "tm", None), P(), P(), P(), P(), P(), P(), P("tm")),
        out_specs=P("elec", "tm", None),
        check_vma=False,
    )
```

```python
import functools
import math

import jax
import jax.numpy as jnp
from jax import lax
from jax.experimental import pallas as pl
from jax.experimental.pallas import tpu as pltpu
from jax.sharding import PartitionSpec as P

WIN = 128
HEADS = 4
INNER = 128
LOG2E = 1.0 / math.log(2.0)
F32 = jnp.float32
BF16 = jnp.bfloat16
MESH = pl.DeviceIdType.MESH
GROUP = 8
EARLY = 1


def dot(a, b):
    return jnp.dot(a, b, preferred_element_type=F32)


def dot_t(a, b):
    return lax.dot_general(a, b, (((1,), (1,)), ((), ())), preferred_element_type=F32)


def split(a):
    high = a.astype(BF16)
    return high, (a - high.astype(F32)).astype(BF16)


def iota(shape, dim):
    return lax.broadcasted_iota(jnp.int32, shape, dim)


def kernel(
    n_tm,
    chunks,
    sig_in,
    wqkv_in,
    wdec_in,
    rate_in,
    gain_in,
    wout_in,
    valid_in,
    bound_in,
    out_ref,
    sig,
    wqkv,
    wout,
    wdec_ref,
    rate_ref,
    gain_ref,
    valid_ref,
    bound_ref,
    wd,
    esig,
    wsig,
    proj,
    ekv,
    eq,
    cum_lanes,
    raw,
    ele,
    msg,
    got,
    local_sem,
    esend,
    erecv,
    wsend,
    wrecv,
    ssend,
    srecv,
):
    elecs, times, width = sig.shape
    hd = INNER // HEADS
    scale = hd**-0.5
    me = lax.axis_index("tm")
    who = lax.axis_index("elec")
    sib = who + 1 - 2 * lax.rem(who, 2)
    far = lax.rem(who + 2, 4)
    far_sib = lax.rem(sib + 2, 4)
    rounds = []
    step = 1
    while step < n_tm:
        rounds.append(step)
        step *= 2
    per = times // chunks

    local = [
        pltpu.make_async_copy(src, dst, local_sem.at[i])
        for i, (src, dst) in enumerate(
            (
                (sig_in, sig),
                (wqkv_in, wqkv),
                (wout_in, wout),
                (wdec_in, wdec_ref),
                (rate_in, rate_ref),
                (gain_in, gain_ref),
                (valid_in, valid_ref),
                (bound_in, bound_ref),
            )
        )
    ]
    for copy in local:
        copy.start()
    barrier = pltpu.get_barrier_semaphore()
    for peer in (sib, far):
        pl.semaphore_signal(barrier, inc=1, device_id={"elec": peer}, device_id_type=MESH)
    targets = 2
    for d in rounds:
        targets = targets + jnp.where(me + d < n_tm, 1, 0)

        @pl.when(me >= d)
        def _():
            pl.semaphore_signal(barrier, inc=1, device_id={"tm": me - d}, device_id_type=MESH)

    @pl.when(me == 0)
    def _():
        wsig[...] = jnp.zeros_like(wsig)

    for r, d in enumerate(rounds):

        @pl.when(me < d)
        def _():
            got[r, : elecs * hd, :] = jnp.zeros((elecs * hd, INNER), BF16)
            got[r, elecs * hd :, :] = jnp.ones((16, INNER), BF16)

    wd[...] = jnp.zeros_like(wd)

    def piece(slot, src, i, peer):
        span = pl.ds(i * per, per)
        return pltpu.make_async_remote_copy(
            src_ref=src.at[:, span, :],
            dst_ref=esig.at[slot, :, span, :],
            send_sem=esend.at[slot, i],
            recv_sem=erecv.at[slot, i],
            device_id={"elec": peer},
            device_id_type=MESH,
        )

    to_sib = [piece(0, sig, i, sib) for i in range(chunks)]
    to_far = [piece(1, sig, i, far) for i in range(chunks)]
    onward = [piece(2, esig.at[1], i, sib) for i in range(chunks)]
    to_next = [
        pltpu.make_async_remote_copy(
            src_ref=sig.at[e],
            dst_ref=wsig.at[e],
            send_sem=wsend.at[e],
            recv_sem=wrecv.at[e],
            device_id={"tm": me + 1},
            device_id_type=MESH,
        )
        for e in range(elecs)
    ]
    states = [
        pltpu.make_async_remote_copy(
            src_ref=msg.at[r],
            dst_ref=got.at[r],
            send_sem=ssend.at[r],
            recv_sem=srecv.at[r],
            device_id={"tm": me + d},
            device_id_type=MESH,
        )
        for r, d in enumerate(rounds)
    ]

    for i in (0, 3, 4, 5, 6, 7):
        local[i].wait()
    wd[:HEADS, :] = wdec_ref[...].astype(F32)

    row = iota((times, INNER), 0)
    lane = iota((times, INNER), 1)
    causal = row >= lane
    lane_head = lane // hd
    flat = sig[...].reshape(elecs * times, width)
    logits_all = dot_t(flat, wd[...].astype(BF16))
    logits = logits_all[:times]
    for e in range(1, elecs):
        logits = logits + pltpu.roll(logits_all[e * times : (e + 1) * times], HEADS * e, 1)
    which = lax.rem(iota((1, INNER), 1), HEADS)
    rates = jnp.zeros((1, INNER), F32)
    for h in range(HEADS):
        rates = jnp.where(which == h, rate_ref[h], rates)
    soft = -2.0 * rates * jax.nn.sigmoid(logits)
    tri = jnp.where(causal, 1.0, 0.0)
    marks = jnp.where(causal, bound_ref[...].reshape(1, times).astype(F32), 0.0).astype(BF16)
    tri16 = tri.astype(BF16)
    soft_hi, soft_mid = split(soft)
    soft_lo = (soft - soft_hi.astype(F32) - soft_mid.astype(F32)).astype(BF16)
    bounds = dot(marks, jnp.ones((times, INNER), BF16))
    cum = dot(tri16, soft_hi) + dot(tri16, soft_mid) + dot(tri16, soft_lo) + math.log(0.5) * bounds
    cum2 = cum * LOG2E
    cum2_t = cum2.T
    pl.semaphore_wait(barrier, targets)
    for i in range(chunks):
        to_far[i].start()
    for i in range(chunks):
        to_sib[i].start()

    def send_window(first, last):
        @pl.when(me + 1 < n_tm)
        def _():
            for copy in to_next[first:last]:
                copy.start()

    send_window(0, EARLY)
    local[1].wait()
    proj[:, :, :384] = dot(flat, wqkv[:, :384]).astype(BF16).reshape(elecs, times, 384)

    block_diag = (row // hd) == lane_head
    inc_state, inc_dec = [], []
    for e in range(elecs):
        spread = jnp.broadcast_to(cum2[:, HEADS * e : HEADS * e + 1], (times, INNER))
        for h in range(1, HEADS):
            at = HEADS * e + h
            spread = jnp.where(
                lane_head == h, jnp.broadcast_to(cum2[:, at : at + 1], (times, INNER)), spread
            )
        cum_lanes[e] = spread
        ending = spread[times - 1 : times, :]
        kept = jnp.exp2(ending - spread)
        high, low = split((proj[e, :, 128:256].astype(F32) * kept).T)
        values = proj[e, :, 256:384]
        full = jnp.where(block_diag, dot(high, values) + dot(low, values), 0.0)
        small = full[:hd]
        for h in range(1, HEADS):
            small = small + full[h * hd : (h + 1) * hd]
        inc_state.append(small)
        inc_dec.append(jnp.exp2(ending))
    exc_state = [jnp.zeros((hd, INNER), F32)] * elecs
    exc_dec = [jnp.ones((1, INNER), F32)] * elecs

    def send_states(r, d):
        for e in range(elecs):
            msg[r, e * hd : (e + 1) * hd, :] = inc_state[e].astype(BF16)
        packed = jnp.broadcast_to(inc_dec[0], (16, INNER))
        for e in range(1, elecs):
            packed = jnp.where(iota((16, INNER), 0) == e, inc_dec[e], packed)
        msg[r, elecs * hd :, :] = packed.astype(BF16)

        @pl.when(me + d < n_tm)
        def _():
            states[r].start()

    def take_states(r, d):
        @pl.when(me >= d)
        def _():
            states[r].wait_recv()

        decs = got[r, elecs * hd :, :].astype(F32)
        for e in range(elecs):
            came = got[r, e * hd : (e + 1) * hd, :].astype(F32)
            dec = decs[e : e + 1]
            exc_state[e] = exc_dec[e] * came + exc_state[e]
            exc_dec[e] = exc_dec[e] * dec
            inc_state[e] = inc_dec[e] * came + inc_state[e]
            inc_dec[e] = inc_dec[e] * dec
        if r + 1 < len(rounds):
            send_states(r + 1, rounds[r + 1])

    send_states(0, rounds[0])
    send_window(EARLY, elecs)

    proj[:, :, 384:768] = dot(flat, wqkv[:, 384:768]).astype(BF16).reshape(elecs, times, 384)
    own = dot(flat, wqkv[:, 768:1152]).astype(BF16).astype(F32).reshape(elecs, times, 384)
    eq[...] = own[:, :, :128]
    ekv[...] = own[:, :, 128:]

    head_row = iota((1, INNER), 1) // hd
    head_masks = [jnp.where(head_row == h, 1.0, 0.0) for h in range(HEADS)]
    masks16 = [m.astype(BF16) for m in head_masks]

    def by_head(query):
        return jnp.concatenate([query * m for m in masks16], axis=0)

    def pick(stacked, rows):
        head = iota((rows, INNER), 1) // hd
        result = stacked[:rows]
        for h in range(1, HEADS):
            result = jnp.where(head == h, stacked[h * rows : (h + 1) * rows], result)
        return result

    def linear(e):
        scores = dot_t(by_head(proj[e, :, :128]), proj[e, :, 128:256])
        weights = []
        for h in range(HEADS):
            at = HEADS * e + h
            gap = cum2[:, at : at + 1] - cum2_t[at : at + 1, :]
            decays = jnp.exp2(jnp.where(causal, gap, -jnp.inf))
            weights.append((scores[h * times : (h + 1) * times] * scale * decays).astype(BF16))
        raw[e] = pick(dot(jnp.concatenate(weights, axis=0), proj[e, :, 256:384]), times)

    fold = scale * LOG2E
    neg = -jnp.inf
    ones_keys = jnp.ones((2 * times, INNER), BF16)

    def window(e):
        @pl.when(me >= 1)
        def _():
            to_next[e].wait_recv()

        prior = dot(wsig[e], wqkv[:, 512:768]).astype(BF16)
        keys = jnp.concatenate([prior[:, :128], proj[e, :, 512:640]], axis=0)
        values = jnp.concatenate([prior[:, 128:], proj[e, :, 640:768]], axis=0)
        scores = dot_t(by_head(proj[e, :, 384:512]), keys)
        before = (lane >= row) & (me > 0)
        weights = []
        for h in range(HEADS):
            part = scores[h * times : (h + 1) * times]
            old = jnp.where(before, part[:, :times], neg)
            new = jnp.where(causal, part[:, times:], neg)
            peak = jnp.max(jnp.maximum(old, new), axis=1, keepdims=True)
            weights.append(
                jnp.concatenate(
                    [
                        jnp.exp2((old - peak) * fold).astype(BF16),
                        jnp.exp2((new - peak) * fold).astype(BF16),
                    ],
                    axis=1,
                )
            )
        both = dot(
            jnp.concatenate(weights, axis=0), jnp.concatenate([values, ones_keys], axis=1)
        )
        return pick(both[:, :128], times) / pick(both[:, 128:], times)

    qrows = elecs * GROUP
    krows = 4 * elecs * GROUP
    erow = iota((HEADS * qrows, krows), 0)
    ecol = iota((HEADS * qrows, krows), 1)
    good = jnp.zeros((1, krows), jnp.int32)
    col_elec = iota((1, krows), 1) // GROUP
    for slot, peer in enumerate((who, sib, far, far_sib)):
        for i in range(elecs):
            good = jnp.where(col_elec == slot * elecs + i, valid_ref[peer * elecs + i], good)
    eallowed = (lax.rem(erow, GROUP) == lax.rem(ecol, GROUP)) & (
        (jnp.broadcast_to(good, ecol.shape) == 1)
        | (ecol // GROUP == lax.rem(erow // GROUP, elecs))
    )
    ones_ele = jnp.ones((krows, INNER), BF16)

    def electrode(i):
        span = pl.ds(i * per, per)
        there = esig[:, :, span, :].reshape(3 * elecs * per, width)
        kv = dot(there, wqkv[:, 896:1152]).astype(BF16).astype(F32)
        kv = kv.reshape(3 * elecs, per, 256)
        for g in range(per // GROUP):
            begin = i * per + g * GROUP
            mine = ekv[:, begin : begin + GROUP, :].reshape(qrows, 256)
            rest = kv[:, g * GROUP : (g + 1) * GROUP, :].reshape(krows - qrows, 256)
            pair = jnp.concatenate([mine, rest], axis=0).astype(BF16)
            query = eq[:, begin : begin + GROUP, :].reshape(qrows, 128).astype(BF16)
            scores = jnp.where(eallowed, dot_t(by_head(query), pair[:, :128]), neg)
            peak = jnp.max(scores, axis=1, keepdims=True)
            weights = jnp.exp2((scores - peak) * fold).astype(BF16)
            both = dot(weights, jnp.concatenate([pair[:, 128:], ones_ele], axis=1))
            result = pick(both[:, :128], qrows) / pick(both[:, 128:], qrows)
            ele[:, begin : begin + GROUP, :] = result.reshape(elecs, GROUP, INNER)

    def forward(i):
        to_far[i].wait_recv()
        onward[i].start()

    def attend(i):
        to_sib[i].wait_recv()
        onward[i].wait_recv()
        electrode(i)

    win = []
    linear(0)
    linear(1)
    forward(0)
    linear(2)
    linear(3)
    forward(1)
    take_states(0, rounds[0])
    win.append(window(0))
    attend(0)
    forward(2)
    if len(rounds) > 1:
        take_states(1, rounds[1])
    win.append(window(1))
    forward(3)
    attend(1)
    win.append(window(2))
    attend(2)
    win.append(window(3))
    for r in range(2, len(rounds)):
        take_states(r, rounds[r])
    gain = gain_ref[...].reshape(1, INNER)
    lin = []
    for e in range(elecs):
        tiled = jnp.concatenate([exc_state[e]] * HEADS, axis=0)
        s_hi, s_lo = split(jnp.where(block_diag, tiled, 0.0))
        q_hi, q_lo = split(proj[e, :, :128].astype(F32) * (jnp.exp2(cum_lanes[e]) * scale))
        total = raw[e] + dot(q_hi, s_hi) + dot(q_hi, s_lo) + dot(q_lo, s_hi)
        square = jnp.mean(total * total, axis=1, keepdims=True)
        lin.append((total * lax.rsqrt(square + 1e-05) * gain).astype(BF16))
    attend(3)
    local[2].wait()
    for e in range(elecs):
        mixed = jnp.concatenate([lin[e], win[e].astype(BF16), ele[e].astype(BF16)], axis=1)
        out_ref[e] = (sig[e].astype(F32) + dot(mixed, wout[...])).astype(BF16)

    for copy in to_sib + to_far + onward:
        copy.wait_send()

    @pl.when(me + 1 < n_tm)
    def _():
        for copy in to_next:
            copy.wait_send()

    for r, d in enumerate(rounds):

        @pl.when(me + d < n_tm)
        def _():
            states[r].wait_send()


def shards(n_tm, signal, w_qkv, w_decay, decay_rate, lin_gain, w_out, valid, boundary):
    elecs, times, width = signal.shape
    hd = INNER // HEADS
    rounds = max(1, (n_tm - 1).bit_length())
    chunks = 4
    hbm = pl.BlockSpec(memory_space=pltpu.HBM)
    dma = pltpu.SemaphoreType.DMA
    return pl.pallas_call(
        functools.partial(kernel, n_tm, chunks),
        out_shape=jax.ShapeDtypeStruct(signal.shape, BF16),
        in_specs=[hbm] * 8,
        out_specs=pl.BlockSpec(memory_space=pltpu.VMEM),
        scratch_shapes=[
            pltpu.VMEM(signal.shape, BF16),
            pltpu.VMEM(w_qkv.shape, BF16),
            pltpu.VMEM(w_out.shape, BF16),
            pltpu.VMEM((HEADS, width), BF16),
            pltpu.SMEM(decay_rate.shape, F32),
            pltpu.VMEM(lin_gain.shape, F32),
            pltpu.SMEM(valid.shape, jnp.int32),
            pltpu.VMEM(boundary.shape, jnp.int32),
            pltpu.VMEM((INNER, width), F32),
            pltpu.VMEM((3, elecs, times, width), BF16),
            pltpu.VMEM((elecs, times, width), BF16),
            pltpu.VMEM((elecs, times, 768), BF16),
            pltpu.VMEM((elecs, times, 256), F32),
            pltpu.VMEM((elecs, times, INNER), F32),
            pltpu.VMEM((elecs, times, INNER), F32),
            pltpu.VMEM((elecs, times, INNER), F32),
            pltpu.VMEM((elecs, times, INNER), F32),
            pltpu.VMEM((rounds, elecs * hd + 16, INNER), BF16),
            pltpu.VMEM((rounds, elecs * hd + 16, INNER), BF16),
            dma((8,)),
            dma((3, chunks)),
            dma((3, chunks)),
            dma((elecs,)),
            dma((elecs,)),
            dma((rounds,)),
            dma((rounds,)),
        ],
        compiler_params=pltpu.CompilerParams(
            collective_id=0, has_side_effects=True
        ),
    )(signal, w_qkv, w_decay.T, decay_rate, lin_gain, w_out, valid, boundary)


def solution(mesh):
    return jax.shard_map(
        functools.partial(shards, mesh.shape["tm"]),
        mesh=mesh,
        in_specs=(P("elec", "tm", None), P(), P(), P(), P(), P(), P(), P("tm")),
        out_specs=P("elec", "tm", None),
        check_vma=False,
    )
```
